256 devices in a mesh: dp: 32 (over y, z_lo, core), mp: 8 (over z_hi, x).
Axes of the slice: x: 4, y: 4, z: 8 (z_hi: 2, z_lo: 4; z = z_hi * 4 + z_lo), core: 2. Of those that a mesh axis runs over, the one named last changes fastest.
Arguments:
- hidden_acts: bfloat16 [2, 16384, 12288], P(None, 'dp', 'mp'), may hold values from -6 to 6
- out_grads: bfloat16 [2, 16384, 3072], P(None, 'dp', 'mp'), may hold values from -6 to 6
- token_picks: int32 [32, 512], P('dp'), may hold values from 0 to 511, each once within a row
- weight_grads: bfloat16 [2, 12288, 3072], P(None, 'dp', 'mp'), may hold values from -6 to 6
Outputs:
- preconditioned: bfloat16 [2, 12288, 3072], P(None, 'dp', 'mp')
The draws below stay inside these ranges and needn't reach their ends.
Inputs may be any that keep to these rules, and one draw needn't show every extreme that they name: `token_picks`: each row is an ordering of 0 to 511; its first 256 entries name the sampled tokens.
All inputs are finite; a program needn't handle non-finite values. Where the reference program divides by a largest or mean magnitude, that divisor is 1e-20 or more.
Results may differ from the reference program's by a relative error of at most 0.0066.
Values may be sent and summed in bfloat16 or wider, within the bound.
A program may use at most 128 MiB of HBM per device.

```python
import jax
import jax.numpy as jnp
from jax import lax

D = 3072
FF = 12288
BLK = 384
LAYERS = 2
ITERS = 5
SAMPLE = 256
POOL = 512
TOKENS = 16384
N_DP = 32


def levels(stream_key, dims, cuts, low, top_value):
    loudness, own = 1.0, jax.random.fold_in(stream_key, 6)
    for dim, blocks in cuts:
        heights = jnp.exp(jax.random.uniform(jax.random.fold_in(own, dim), (blocks,), jnp.float32, low / len(cuts), top_value / len(cuts)))
        loudness = loudness * jnp.repeat(heights, dims[dim] // blocks).reshape([-1 if axis == dim else 1 for axis in range(len(dims))])
    return loudness


def gaussian(own_key, dims, spread, reach, split=(), held_as=jnp.bfloat16):
    values = spread * jax.random.normal(own_key, dims, jnp.float32)
    if split:
        values = values * levels(own_key, dims, split, -0.22, 0.18)
    return jnp.clip(values, -reach, reach).astype(held_as)


def setup_inputs(seed: int = 0) -> dict:
    keys = jax.random.split(jax.random.key(seed), 5)
    hidden_acts = gaussian(keys[0], (LAYERS, TOKENS, FF), 1.0, 6.0, ((1, 32), (2, 8)))
    out_grads = gaussian(keys[1], (LAYERS, TOKENS, D), 1.0, 6.0, ((1, 32), (2, 8)))
    token_picks = jax.vmap(lambda own: jax.random.permutation(own, POOL))(jax.random.split(keys[2], N_DP)).reshape((N_DP, POOL)).astype(jnp.int32)
    weight_grads = gaussian(keys[3], (LAYERS, FF, D), 1.0, 6.0, ((1, 32), (2, 8)))
    return dict(hidden_acts=hidden_acts, out_grads=out_grads, token_picks=token_picks, weight_grads=weight_grads)


damping = 0.1
highest = lax.Precision.HIGHEST


def batched(first, second):
    return jnp.einsum("kab,kbc->kac", first, second, precision=highest, preferred_element_type=jnp.float32)


def newton_full(factor):
    row_bound = jnp.max(jnp.sum(jnp.abs(factor), axis=-1), axis=-1)
    identity = jnp.eye(factor.shape[-1], dtype=jnp.float32)
    approx = identity[None] / row_bound[:, None, None]
    for sweep in range(ITERS):
        approx = 2.0 * approx - batched(approx, batched(factor, approx))
    return approx


def sample_rows(acts, picks):
    row_ids = picks[:, :SAMPLE] + (jnp.arange(N_DP, dtype=jnp.int32) * POOL)[:, None]
    return jnp.take(acts, row_ids.reshape(-1).astype(jnp.int32), axis=1)


def build_factor(chosen):
    tile_stack = chosen.astype(jnp.float32).reshape(LAYERS, chosen.shape[1], -1, BLK)
    gram_sum = jnp.einsum("lsta,lstb->ltab", tile_stack, tile_stack, precision=highest, preferred_element_type=jnp.float32)
    identity = jnp.eye(BLK, dtype=jnp.float32)
    return gram_sum / (SAMPLE * N_DP) + damping * identity


def reference(hidden_acts, out_grads, token_picks, weight_grads):
    a_factor = build_factor(sample_rows(hidden_acts, token_picks))
    g_factor = build_factor(sample_rows(out_grads, token_picks))
    a_inverse = newton_full(a_factor.reshape(-1, BLK, BLK)).astype(jnp.bfloat16).reshape(a_factor.shape)
    g_inverse = newton_full(g_factor.reshape(-1, BLK, BLK)).astype(jnp.bfloat16).reshape(g_factor.shape)
    grad_tiles = weight_grads.astype(jnp.float32).reshape(LAYERS, FF // BLK, BLK, D // BLK, BLK)
    left_product = jnp.einsum("lrab,lrbcd->lracd", a_inverse.astype(jnp.float32), grad_tiles, precision=highest, preferred_element_type=jnp.float32).astype(jnp.bfloat16)
    result = jnp.einsum("lracd,lcde->lrace", left_product.astype(jnp.float32), g_inverse.astype(jnp.float32), precision=highest, preferred_element_type=jnp.float32).astype(jnp.bfloat16)
    return result.reshape(LAYERS, FF, D)
```

```python
import jax
import jax.numpy as jnp
from jax import lax
from jax.experimental import pallas as pl
from jax.experimental.pallas import tpu as pltpu
from jax.sharding import PartitionSpec as P

BLK = 384
SAMPLE = 256
POOL = 512
ROWS = 768
PART = 192
DAMPING = 0.1
MESH = pl.DeviceIdType.MESH
F32 = jnp.float32
BF16 = jnp.bfloat16
GROUPS = ((0, 2), (2, 2), (4, 1))
BLOCKS = ((0, 0), (0, 1), (0, 2), (1, 1), (1, 2), (2, 2))


def kernel(
    hid_hbm, grd_hbm, picks, w_hbm, out,
    hid, grd, wv, mask, abuf, arec, own, s1, brec, ysum, cs, crec, grec, dtot, gtot, ft, lhs, rhs, acc, ginv, left,
    load_sem, a_s, a_r, b_s, b_r, c_s, c_r, g_s, g_r, d_s, d_r, e_s, e_r, h_s, h_r, i_s, i_r,
):
    i, m = lax.axis_index("dp"), lax.axis_index("mp")
    c, z, y = lax.rem(i, 2), lax.rem(i // 2, 4), i // 8
    zh, x = m // 4, lax.rem(m, 4)
    active = z // 2 == lax.rem(x, 2)
    x_src = lax.rem(y, 2) * 2 + z // 2

    def dev(y=y, z=z, c=c, zh=zh, x=x):
        return ((y * 4 + z) * 2 + c, zh * 4 + x)

    def turn(v, by):
        return lax.rem(v + by, 4)

    def send(src, dst, ss, rs, to):
        return pltpu.make_async_remote_copy(
            src_ref=src, dst_ref=dst, send_sem=ss, recv_sem=rs, device_id=to, device_id_type=MESH
        )

    def part(q):
        return pl.ds(pl.multiple_of(q * PART, PART), PART)

    barrier = pltpu.get_barrier_semaphore()

    def greet(to):
        pl.semaphore_signal(barrier, inc=1, device_id=to, device_id_type=MESH)

    greet(dev(c=1 - c))
    greet(dev(zh=1 - zh))
    for by in (1, 2, 3):
        greet(dev(y=turn(y, by)))
        greet(dev(z=turn(z, by)))
    for cc in (0, 1):
        for by in range(4):
            if by:
                greet(dev(x=x_src, y=turn(y, by), c=cc))
            else:
                @pl.when((x_src != x) | (c != cc))
                def _():
                    greet(dev(x=x_src, c=cc))

    other = 1 - c
    loads = []
    for n, (src, dst) in enumerate((
        (hid_hbm.at[other], hid.at[other]), (grd_hbm.at[other], grd.at[other]),
        (hid_hbm.at[c], hid.at[c]), (grd_hbm.at[c], grd.at[c]), (w_hbm, wv),
    )):
        loads.append(pltpu.make_async_copy(src, dst, load_sem.at[n]))
        loads[-1].start()

    token = lax.broadcasted_iota(jnp.int32, (POOL, SAMPLE), 0)
    hit = jnp.where(token == picks[:, :SAMPLE], 1.0, 0.0)
    mask[...] = jnp.broadcast_to(jnp.max(hit, axis=1, keepdims=True), (POOL, BLK)).astype(BF16)

    def gram(tile, dst):
        masked = tile * mask[...]
        row = 0
        for r in range(3):
            g = lax.dot_general(
                masked[:, r * 128 : (r + 1) * 128], tile[:, r * 128 :], (((0,), (0,)), ((), ())),
                preferred_element_type=F32,
            )
            for k in range(3 - r):
                dst[row : row + 128, :] = g[:, k * 128 : (k + 1) * 128].astype(dst.dtype)
                row += 128

    def grams(layer, first, count, dst):
        if count == 1:
            gram(grd[layer], dst.at[first])
        else:
            def body(t, _):
                gram(hid[layer, :, pl.ds(pl.multiple_of(t * BLK, 128), BLK)], dst.at[t])
                return 0

            lax.fori_loop(first, first + count, body, 0)

    started = []
    for g, (first, count) in enumerate(GROUPS):
        if g != 1:
            loads[0 if g == 0 else 1].wait()
        grams(other, first, count, abuf)
        if g == 0:
            pl.semaphore_wait(barrier, 8 + jnp.where(active, jnp.where(lax.rem(y, 2) == x // 2, 15, 16), 0))
        span = pl.ds(first, count)
        copy = send(abuf.at[span], arec.at[span], a_s.at[g], a_r.at[g], dev(c=other))
        copy.start()
        started.append(copy)
    loads[2].wait()
    loads[3].wait()
    for first, count in GROUPS:
        grams(c, first, count, own)

    from_sibling = list(started)
    from_y = {}
    for g, (first, count) in enumerate(GROUPS):
        from_sibling[g].wait_recv()
        for t in range(first, first + count):
            total = own[t] + arec[t].astype(F32)
            own[t] = total
            s1[t] = total.astype(BF16)
        span = pl.ds(first, count)
        for by in (1, 2, 3):
            to = turn(y, by)
            copy = send(
                s1.at[span, part(to)], brec.at[by - 1, span], b_s.at[g, by - 1], b_r.at[g, by - 1], dev(y=to)
            )
            copy.start()
            started.append(copy)
            from_y[g, by] = copy

    from_z = {}
    for g, (first, count) in enumerate(GROUPS):
        for by in (1, 2, 3):
            from_y[g, by].wait_recv()
        for t in range(first, first + count):
            total = own[t, part(y)]
            for by in (1, 2, 3):
                total += brec[by - 1, t].astype(F32)
            ysum[t] = total
            cs[t] = total.astype(BF16)
        if g < 2:
            goal = 2 * lax.rem(x, 2) + g

            @pl.when(z != goal)
            def _():
                slot = lax.rem(z - goal + 4, 4) - 1
                send(cs.at[pl.ds(first, 2)], crec.at[slot], c_s.at[g], c_r.at[slot], dev(z=goal)).start()
        else:
            for by in (1, 2, 3):
                copy = send(cs.at[4], grec.at[by - 1], g_s.at[by - 1], g_r.at[by - 1], dev(z=turn(z, by)))
                copy.start()
                started.append(copy)
                from_z[by] = copy

    def spread(plane):
        y_goal = plane * 2 + x // 2
        for e in (0, 1):
            for by in range(4):
                copy = send(
                    dtot.at[plane, e], ft.at[c, part(y)], e_s.at[plane, e, by], e_r.at[c, y],
                    dev(y=y_goal, c=e, x=turn(x, by)),
                )
                if by:
                    copy.start()
                else:
                    here = (y_goal == y) & (c == e)

                    @pl.when(here)
                    def _():
                        ft[c, part(y)] = dtot[plane, e]

                    @pl.when(jnp.logical_not(here))
                    def _():
                        copy.start()

    cross = send(dtot.at[zh], dtot.at[zh], d_s, d_r, dev(zh=1 - zh))

    @pl.when(active)
    def _():
        for by in (1, 2, 3):
            send(cs.at[pl.ds(0, 2)], crec.at[by - 1], c_s.at[0], c_r.at[by - 1], dev(c=other)).wait_recv()
        for e in (0, 1):
            total = ysum[2 * lax.rem(z, 2) + e]
            for by in (1, 2, 3):
                total += crec[by - 1, e].astype(F32)
            dtot[zh, e] = total.astype(BF16)
        cross.start()
        spread(zh)

    for by in (1, 2, 3):
        from_z[by].wait_recv()
    total = ysum[4]
    for by in (1, 2, 3):
        total += grec[by - 1].astype(F32)
    gtot[...] = total.astype(BF16)
    ft[2, part(y)] = gtot[...]
    for by in (1, 2, 3):
        copy = send(gtot, ft.at[2, part(y)], h_s.at[by - 1], h_r.at[by - 1], dev(y=turn(y, by)))
        copy.start()
        started.append(copy)

    @pl.when(active)
    def _():
        send(dtot.at[zh], dtot.at[1 - zh], d_s, d_r, dev(zh=1 - zh)).wait_recv()
        spread(1 - zh)

    def inverse(slot):
        block = {rc: ft[slot, n * 128 : (n + 1) * 128].astype(F32) for n, rc in enumerate(BLOCKS)}
        for r in range(3):
            for k in range(3):
                tile = block[r, k] if r <= k else block[k, r].T
                acc[r * 128 : (r + 1) * 128, k * 128 : (k + 1) * 128] = tile
        eye = jnp.where(
            lax.broadcasted_iota(jnp.int32, (BLK, BLK), 0) == lax.broadcasted_iota(jnp.int32, (BLK, BLK), 1), 1.0, 0.0
        )
        factor = acc[...] * (1.0 / 8192.0) + DAMPING * eye
        bound = jnp.max(jnp.sum(jnp.abs(factor), axis=1, keepdims=True), axis=0, keepdims=True)
        step = 1.0 / bound

        def put(value, column):
            high = value.astype(BF16)
            low = (value - high.astype(F32)).astype(BF16)
            span = slice(column * BLK, (column + 1) * BLK)
            rhs[0:BLK, span] = high
            rhs[BLK : 2 * BLK, span] = low
            rhs[2 * BLK :, span] = high
            if column == 0:
                lhs[:, 0:BLK] = high
                lhs[:, BLK : 2 * BLK] = high
                lhs[:, 2 * BLK :] = low

        residue = eye - factor * step
        acc[...] = eye + residue
        put(residue, 0)
        put(acc[...], 1)
        put(jnp.dot(lhs[...], rhs[:, :BLK], preferred_element_type=F32), 0)
        for _ in range(3):
            both = jnp.dot(lhs[...], rhs[...], preferred_element_type=F32)
            acc[...] += both[:, BLK:]
            put(both[:, :BLK], 0)
            put(acc[...], 1)
        acc[...] += jnp.dot(lhs[...], rhs[:, BLK:], preferred_element_type=F32)
        return (acc[...] * step).astype(BF16)

    for by in (1, 2, 3):
        send(gtot, ft.at[2, part(y)], h_s.at[by - 1], h_r.at[by - 1], dev(y=turn(y, by))).wait_recv()
    ginv[c] = inverse(2)
    swap = send(ginv.at[c], ginv.at[c], i_s, i_r, dev(c=other))
    swap.start()
    loads[4].wait()

    def layer_step(layer, _):
        for yy in range(4):
            mine = (x == x_src) & (c == layer) & (y == yy)

            @pl.when(jnp.logical_not(mine))
            def _():
                send(
                    dtot.at[0, 0], ft.at[layer, part(yy)], e_s.at[0, 0, 0], e_r.at[layer, yy], dev(c=other)
                ).wait_recv()
        left[layer] = jnp.dot(inverse(layer), wv[layer], preferred_element_type=F32).astype(BF16)
        return 0

    lax.fori_loop(0, 2, layer_step, 0)
    swap.wait()
    for layer in (0, 1):
        out[layer] = jnp.dot(left[layer], ginv[layer], preferred_element_type=F32).astype(BF16)

    for copy in started:
        copy.wait_send()
    for g in (0, 1):
        @pl.when(z != 2 * lax.rem(x, 2) + g)
        def _():
            send(cs.at[pl.ds(0, 2)], crec.at[0], c_s.at[g], c_r.at[0], dev(c=other)).wait_send()

    @pl.when(active)
    def _():
        cross.wait_send()
        for plane in (0, 1):
            for e in (0, 1):
                for by in range(4):
                    copy = send(dtot.at[0, 0], ft.at[0, part(0)], e_s.at[plane, e, by], e_r.at[0, 0], dev(c=other))
                    if by:
                        copy.wait_send()
                    else:
                        @pl.when((plane * 2 + x // 2 != y) | (c != e))
                        def _():
                            copy.wait_send()


def shards(hidden_acts, out_grads, token_picks, weight_grads):
    dma = pltpu.SemaphoreType.DMA
    vmem = pltpu.VMEM
    return pl.pallas_call(
        kernel,
        out_shape=jax.ShapeDtypeStruct(weight_grads.shape, BF16),
        in_specs=[
            pl.BlockSpec(memory_space=pl.ANY),
            pl.BlockSpec(memory_space=pl.ANY),
            pl.BlockSpec(memory_space=vmem),
            pl.BlockSpec(memory_space=pl.ANY),
        ],
        out_specs=pl.BlockSpec(memory_space=vmem),
        scratch_shapes=[
            vmem(hidden_acts.shape, BF16), vmem(out_grads.shape, BF16), vmem(weight_grads.shape, BF16),
            vmem((POOL, BLK), BF16),
            vmem((5, ROWS, 128), BF16), vmem((5, ROWS, 128), BF16), vmem((5, ROWS, 128), F32), vmem((5, ROWS, 128), BF16),
            vmem((3, 5, PART, 128), BF16), vmem((5, PART, 128), F32), vmem((5, PART, 128), BF16),
            vmem((3, 2, PART, 128), BF16), vmem((3, PART, 128), BF16), vmem((2, 2, PART, 128), BF16),
            vmem((PART, 128), BF16), vmem((3, ROWS, 128), BF16),
            vmem((BLK, 3 * BLK), BF16), vmem((3 * BLK, 2 * BLK), BF16), vmem((BLK, BLK), F32),
            vmem((2, BLK, BLK), BF16), vmem((2, BLK, BLK), BF16),
            dma((5,)), dma((3,)), dma((3,)), dma((3, 3)), dma((3, 3)), dma((2,)), dma((3,)), dma((3,)), dma((3,)),
            dma, dma, dma((2, 2, 4)), dma((2, 4)), dma((3,)), dma((3,)), dma, dma,
        ],
        compiler_params=pltpu.CompilerParams(
            collective_id=0, has_side_effects=True, vmem_limit_bytes=48 * 2**20
        ),
    )(hidden_acts, out_grads, token_picks, weight_grads)


def solution(mesh):
    placed = (P(None, "dp", "mp"), P(None, "dp", "mp"), P("dp", None), P(None, "dp", "mp"))
    return jax.shard_map(shards, mesh=mesh, in_specs=placed, out_specs=P(None, "dp", "mp"), check_vma=False)
```

```python
import jax
import jax.numpy as jnp
from jax import lax
from jax.experimental import pallas as pl
from jax.experimental.pallas import tpu as pltpu
from jax.sharding import PartitionSpec as P

BLK = 384
SAMPLE = 256
POOL = 512
ROWS = 768
PART = 192
DAMPING = 0.1
MESH = pl.DeviceIdType.MESH
F32 = jnp.float32
BF16 = jnp.bfloat16
ORDER = (0, 2, 4, 1, 3)
BLOCKS = ((0, 0), (0, 1), (0, 2), (1, 1), (1, 2), (2, 2))


def kernel(
    hid_hbm, grd_hbm, picks, w_hbm, out,
    hid, grd, wv, mask, abuf, arec, own, s1, brec, ysum, cs, crec, grec, dtot, gtot, ft, lhs, rhs, acc, ginv, left,
    load_sem, a_s, a_r, b_s, b_r, c_s, c_r, g_s, g_r, d_s, d_r, e_s, e_r, h_s, h_r, i_s, i_r,
):
    i, m = lax.axis_index("dp"), lax.axis_index("mp")
    c, z, y = lax.rem(i, 2), lax.rem(i // 2, 4), i // 8
    zh, x = m // 4, lax.rem(m, 4)
    active = z // 2 == lax.rem(x, 2)
    x_src = lax.rem(y, 2) * 2 + z // 2

    def dev(y=y, z=z, c=c, zh=zh, x=x):
        return ((y * 4 + z) * 2 + c, zh * 4 + x)

    def turn(v, by):
        return lax.rem(v + by, 4)

    def send(src, dst, ss, rs, to):
        return pltpu.make_async_remote_copy(
            src_ref=src, dst_ref=dst, send_sem=ss, recv_sem=rs, device_id=to, device_id_type=MESH
        )

    def part(q):
        return pl.ds(pl.multiple_of(q * PART, PART), PART)

    barrier = pltpu.get_barrier_semaphore()

    def greet(to):
        pl.semaphore_signal(barrier, inc=1, device_id=to, device_id_type=MESH)

    greet(dev(c=1 - c))
    greet(dev(zh=1 - zh))
    for by in (1, 2, 3):
        greet(dev(y=turn(y, by)))
        greet(dev(z=turn(z, by)))
    for cc in (0, 1):
        for by in range(4):
            if by:
                greet(dev(x=x_src, y=turn(y, by), c=cc))
            else:
                @pl.when((x_src != x) | (c != cc))
                def _():
                    greet(dev(x=x_src, c=cc))

    other = 1 - c
    loads = {}
    for n, (own_layer, t) in enumerate([(own_layer, t) for own_layer in (0, 1) for t in ORDER]):
        layer = c if own_layer else other
        if t == 4:
            copy = pltpu.make_async_copy(grd_hbm.at[layer], grd.at[layer], load_sem.at[n])
        else:
            span = pl.ds(t * BLK, BLK)
            copy = pltpu.make_async_copy(hid_hbm.at[layer, :, span], hid.at[layer, :, span], load_sem.at[n])
        copy.start()
        loads[own_layer, t] = copy
    load_w = pltpu.make_async_copy(w_hbm, wv, load_sem.at[10])
    load_w.start()

    token = lax.broadcasted_iota(jnp.int32, (POOL, SAMPLE), 0)
    hit = jnp.where(token == picks[:, :SAMPLE], 1.0, 0.0)
    mask[...] = jnp.broadcast_to(jnp.max(hit, axis=1, keepdims=True), (POOL, BLK)).astype(BF16)

    def gram(tile, dst):
        masked = tile * mask[...]
        row = 0
        for r in range(3):
            g = lax.dot_general(
                masked[:, r * 128 : (r + 1) * 128], tile[:, r * 128 :], (((0,), (0,)), ((), ())),
                preferred_element_type=F32,
            )
            for k in range(3 - r):
                dst[row : row + 128, :] = g[:, k * 128 : (k + 1) * 128].astype(dst.dtype)
                row += 128

    def gram_of(own_layer, t, dst):
        loads[own_layer, t].wait()
        layer = c if own_layer else other
        gram(grd[layer] if t == 4 else hid[layer, :, t * BLK : (t + 1) * BLK], dst.at[t])

    started, from_sibling, from_y, from_z = [], {}, {}, {}
    for n, t in enumerate(ORDER):
        gram_of(0, t, abuf)
        if n == 0:
            pl.semaphore_wait(barrier, 8 + jnp.where(active, jnp.where(lax.rem(y, 2) == x // 2, 15, 16), 0))
        copy = send(abuf.at[t], arec.at[t], a_s.at[t], a_r.at[t], dev(c=other))
        copy.start()
        started.append(copy)
        from_sibling[t] = copy
    for t in ORDER:
        gram_of(1, t, own)

    for t in ORDER:
        from_sibling[t].wait_recv()
        total = own[t] + arec[t].astype(F32)
        own[t] = total
        s1[t] = total.astype(BF16)
        for by in (2, 1, 3):
            to = turn(y, by)
            copy = send(s1.at[t, part(to)], brec.at[by - 1, t], b_s.at[t, by - 1], b_r.at[t, by - 1], dev(y=to))
            copy.start()
            started.append(copy)
            from_y[t, by] = copy

    def sum_y(t):
        for by in (1, 2, 3):
            from_y[t, by].wait_recv()
        total = own[t, part(y)]
        for by in (1, 2, 3):
            total += brec[by - 1, t].astype(F32)
        ysum[t] = total
        cs[t] = total.astype(BF16)

    def to_users(t):
        sum_y(t)
        goal = 2 * lax.rem(x, 2) + t // 2

        @pl.when(z != goal)
        def _():
            slot = lax.rem(z - goal + 4, 4) - 1
            send(cs.at[t], crec.at[slot, t % 2], c_s.at[t], c_r.at[slot, t % 2], dev(z=goal)).start()

    def spread(plane, e):
        y_goal = plane * 2 + x // 2
        for by in (2, 1, 3, 0):
            copy = send(
                dtot.at[plane, e], ft.at[c, part(y)], e_s.at[plane, e, by], e_r.at[c, y],
                dev(y=y_goal, c=e, x=turn(x, by)),
            )
            if by:
                copy.start()
            else:
                here = (y_goal == y) & (c == e)

                @pl.when(here)
                def _():
                    ft[c, part(y)] = dtot[plane, e]

                @pl.when(jnp.logical_not(here))
                def _():
                    copy.start()

    def cross(e):
        return send(dtot.at[zh, e], dtot.at[zh, e], d_s.at[e], d_r.at[e], dev(zh=1 - zh))

    def own_plane(e):
        @pl.when(active)
        def _():
            for by in (1, 2, 3):
                send(cs.at[0], crec.at[by - 1, e], c_s.at[0], c_r.at[by - 1, e], dev(c=other)).wait_recv()
            total = ysum[2 * lax.rem(z, 2) + e]
            for by in (1, 2, 3):
                total += crec[by - 1, e].astype(F32)
            dtot[zh, e] = total.astype(BF16)
            cross(e).start()
            spread(zh, e)

    def other_plane(e):
        @pl.when(active)
        def _():
            send(dtot.at[zh, e], dtot.at[1 - zh, e], d_s.at[e], d_r.at[e], dev(zh=1 - zh)).wait_recv()
            spread(1 - zh, e)

    to_users(0)
    to_users(2)
    sum_y(4)
    for by in (1, 2, 3):
        copy = send(cs.at[4], grec.at[by - 1], g_s.at[by - 1], g_r.at[by - 1], dev(z=turn(z, by)))
        copy.start()
        started.append(copy)
        from_z[by] = copy
    own_plane(0)
    to_users(1)
    to_users(3)
    other_plane(0)
    for by in (1, 2, 3):
        from_z[by].wait_recv()
    total = ysum[4]
    for by in (1, 2, 3):
        total += grec[by - 1].astype(F32)
    gtot[...] = total.astype(BF16)
    ft[2, part(y)] = gtot[...]
    for by in (1, 2, 3):
        copy = send(gtot, ft.at[2, part(y)], h_s.at[by - 1], h_r.at[by - 1], dev(y=turn(y, by)))
        copy.start()
        started.append(copy)
    own_plane(1)
    other_plane(1)

    eye = jnp.where(
        lax.broadcasted_iota(jnp.int32, (BLK, BLK), 0) == lax.broadcasted_iota(jnp.int32, (BLK, BLK), 1), 1.0, 0.0
    )

    def put(slot, value, column):
        high = value.astype(BF16)
        low = (value - high.astype(F32)).astype(BF16)
        span = slice(column * BLK, (column + 1) * BLK)
        rhs[slot, 0:BLK, span] = high
        rhs[slot, BLK : 2 * BLK, span] = low
        rhs[slot, 2 * BLK :, span] = high
        if column == 0:
            lhs[slot, :, 0:BLK] = high
            lhs[slot, :, BLK : 2 * BLK] = high
            lhs[slot, :, 2 * BLK :] = low

    def dot(a, b):
        return jnp.dot(a, b, preferred_element_type=F32)

    def inverses(slots):
        scale = {}
        for s in slots:
            block = {rc: ft[s, n * 128 : (n + 1) * 128].astype(F32) for n, rc in enumerate(BLOCKS)}
            for r in range(3):
                for k in range(3):
                    tile = block[r, k] if r <= k else block[k, r].T
                    acc[s, r * 128 : (r + 1) * 128, k * 128 : (k + 1) * 128] = tile
        for s in slots:
            factor = acc[s] * (1.0 / 8192.0) + DAMPING * eye
            bound = jnp.max(jnp.sum(jnp.abs(factor), axis=1, keepdims=True), axis=0, keepdims=True)
            scale[s] = 1.0 / bound
            residue = eye - factor * scale[s]
            acc[s] = eye + residue
            put(s, residue, 0)
            put(s, acc[s], 1)
        for s in slots:
            put(s, dot(lhs[s], rhs[s, :, :BLK]), 0)
        for _ in range(2):
            for s in slots:
                both = dot(lhs[s], rhs[s])
                acc[s] += both[:, BLK:]
                put(s, both[:, :BLK], 0)
                put(s, acc[s], 1)
        for s in slots:
            acc[s] += dot(lhs[s], rhs[s, :, BLK:])
            square = dot(lhs[s, :, :BLK], rhs[s, :BLK, :BLK]).astype(BF16)
            acc[s] += dot(square, acc[s].astype(BF16))
        return [(acc[s] * scale[s]).astype(BF16) for s in slots]

    for by in (1, 2, 3):
        send(gtot, ft.at[2, part(y)], h_s.at[by - 1], h_r.at[by - 1], dev(y=turn(y, by))).wait_recv()
    ginv[c] = inverses((2,))[0]
    swap = send(ginv.at[c], ginv.at[c], i_s, i_r, dev(c=other))
    swap.start()
    load_w.wait()
    for layer in (0, 1):
        for yy in range(4):
            mine = (x == x_src) & (c == layer) & (y == yy)

            @pl.when(jnp.logical_not(mine))
            def _():
                send(
                    dtot.at[0, 0], ft.at[layer, part(yy)], e_s.at[0, 0, 0], e_r.at[layer, yy], dev(c=other)
                ).wait_recv()
    for layer, inverse in enumerate(inverses((0, 1))):
        left[layer] = dot(inverse, wv[layer]).astype(BF16)
    swap.wait()
    for layer in (0, 1):
        out[layer] = dot(left[layer], ginv[layer]).astype(BF16)

    for copy in started:
        copy.wait_send()
    for t in range(4):
        @pl.when(z != 2 * lax.rem(x, 2) + t // 2)
        def _():
            send(cs.at[0], crec.at[0, 0], c_s.at[t], c_r.at[0, 0], dev(c=other)).wait_send()

    @pl.when(active)
    def _():
        for e in (0, 1):
            cross(e).wait_send()
        for plane in (0, 1):
            for e in (0, 1):
                for by in range(4):
                    copy = send(dtot.at[0, 0], ft.at[0, part(0)], e_s.at[plane, e, by], e_r.at[0, 0], dev(c=other))
                    if by:
                        copy.wait_send()
                    else:
                        @pl.when((plane * 2 + x // 2 != y) | (c != e))
                        def _():
                            copy.wait_send()


def shards(hidden_acts, out_grads, token_picks, weight_grads):
    dma = pltpu.SemaphoreType.DMA
    vmem = pltpu.VMEM
    return pl.pallas_call(
        kernel,
        out_shape=jax.ShapeDtypeStruct(weight_grads.shape, BF16),
        in_specs=[
            pl.BlockSpec(memory_space=pl.ANY),
            pl.BlockSpec(memory_space=pl.ANY),
            pl.BlockSpec(memory_space=vmem),
            pl.BlockSpec(memory_space=pl.ANY),
        ],
        out_specs=pl.BlockSpec(memory_space=vmem),
        scratch_shapes=[
            vmem(hidden_acts.shape, BF16), vmem(out_grads.shape, BF16), vmem(weight_grads.shape, BF16),
            vmem((POOL, BLK), BF16),
            vmem((5, ROWS, 128), BF16), vmem((5, ROWS, 128), BF16), vmem((5, ROWS, 128), F32), vmem((5, ROWS, 128), BF16),
            vmem((3, 5, PART, 128), BF16), vmem((5, PART, 128), F32), vmem((5, PART, 128), BF16),
            vmem((3, 2, PART, 128), BF16), vmem((3, PART, 128), BF16), vmem((2, 2, PART, 128), BF16),
            vmem((PART, 128), BF16), vmem((3, ROWS, 128), BF16),
            vmem((3, BLK, 3 * BLK), BF16), vmem((3, 3 * BLK, 2 * BLK), BF16), vmem((3, BLK, BLK), F32),
            vmem((2, BLK, BLK), BF16), vmem((2, BLK, BLK), BF16),
            dma((11,)), dma((5,)), dma((5,)), dma((5, 3)), dma((5, 3)), dma((4,)), dma((3, 2)), dma((3,)), dma((3,)),
            dma((2,)), dma((2,)), dma((2, 2, 4)), dma((2, 4)), dma((3,)), dma((3,)), dma, dma,
        ],
        compiler_params=pltpu.CompilerParams(
            collective_id=0, has_side_effects=True, vmem_limit_bytes=58 * 2**20
        ),
    )(hidden_acts, out_grads, token_picks, weight_grads)


def solution(mesh):
    placed = (P(None, "dp", "mp"), P(None, "dp", "mp"), P("dp", None), P(None, "dp", "mp"))
    return jax.shard_map(shards, mesh=mesh, in_specs=placed, out_specs=P(None, "dp", "mp"), check_vma=False)
```

```python
import jax
import jax.numpy as jnp
from jax import lax
from jax.experimental import pallas as pl
from jax.experimental.pallas import tpu as pltpu
from jax.sharding import PartitionSpec as P

BLK = 384
SAMPLE = 256
POOL = 512
ROWS = 640
PART = 160
DAMPING = 0.1
MESH = pl.DeviceIdType.MESH
F32 = jnp.float32
BF16 = jnp.bfloat16
ORDER = (0, 2, 4, 1, 3)


def kernel(
    hid_hbm, grd_hbm, picks, w_hbm, out,
    hid, grd, wv, mask, abuf, arec, own, s1, brec, ysum, cs, crec, grec, dtot, gtot, ft, lhs, rhs, acc, ginv, left,
    load_sem, a_s, a_r, b_s, b_r, c_s, c_r, g_s, g_r, d_s, d_r, e_s, e_r, h_s, h_r, i_s, i_r,
):
    i, m = lax.axis_index("dp"), lax.axis_index("mp")
    c, z, y = lax.rem(i, 2), lax.rem(i // 2, 4), i // 8
    zh, x = m // 4, lax.rem(m, 4)
    active = z // 2 == lax.rem(x, 2)
    x_pair = x + 1 - 2 * lax.rem(x, 2)
    x_src = lax.rem(y, 2) * 2 + z // 2
    x_from = jnp.where(zh == y // 2, x_src, x_src + 1 - 2 * lax.rem(x_src, 2))
    y_goal = jnp.where(active, zh, 1 - zh) * 2 + x // 2

    def dev(y=y, z=z, c=c, zh=zh, x=x):
        return ((y * 4 + z) * 2 + c, zh * 4 + x)

    def turn(v, by):
        return lax.rem(v + by, 4)

    def send(src, dst, ss, rs, to):
        return pltpu.make_async_remote_copy(
            src_ref=src, dst_ref=dst, send_sem=ss, recv_sem=rs, device_id=to, device_id_type=MESH
        )

    def part(q):
        return pl.ds(pl.multiple_of(q * PART, PART), PART)

    other = 1 - c
    loads = {}
    for n, (t, own_layer) in enumerate([(t, own_layer) for t in ORDER for own_layer in (0, 1)]):
        layer = c if own_layer else other
        if t == 4:
            copy = pltpu.make_async_copy(grd_hbm.at[layer], grd.at[layer], load_sem.at[n])
        else:
            span = pl.ds(t * BLK, BLK)
            copy = pltpu.make_async_copy(hid_hbm.at[layer, :, span], hid.at[layer, :, span], load_sem.at[n])
        copy.start()
        loads[own_layer, t] = copy
    load_w = pltpu.make_async_copy(w_hbm, wv, load_sem.at[10])
    load_w.start()

    barrier = pltpu.get_barrier_semaphore()

    def greet(to):
        pl.semaphore_signal(barrier, inc=1, device_id=to, device_id_type=MESH)

    greet(dev(c=1 - c))
    greet(dev(zh=1 - zh, x=x_pair))
    for by in (1, 2, 3):
        greet(dev(y=turn(y, by)))
        greet(dev(z=turn(z, by)))
    for cc in (0, 1):
        for by in range(4):
            if by:
                greet(dev(x=x_from, y=turn(y, by), c=cc))
            else:
                @pl.when((x_from != x) | (c != cc))
                def _():
                    greet(dev(x=x_from, c=cc))

    token = lax.broadcasted_iota(jnp.int32, (POOL, SAMPLE), 0)
    hit = jnp.where(token == picks[:, :SAMPLE], 1.0, 0.0)
    mask[...] = jnp.broadcast_to(jnp.max(hit, axis=1, keepdims=True), (POOL, BLK)).astype(BF16)

    row = lax.broadcasted_iota(jnp.int32, (128, 128), 0)
    col = lax.broadcasted_iota(jnp.int32, (128, 128), 1)

    def diagonal(block):
        return jnp.sum(jnp.where(row == col, block, 0.0), axis=0, keepdims=True)

    def gram(tile, dst):
        masked = tile * mask[...]
        g0, g1, g2 = [
            lax.dot_general(
                masked[:, r * 128 : (r + 1) * 128], tile[:, r * 128 :], (((0,), (0,)), ((), ())),
                preferred_element_type=F32,
            )
            for r in range(3)
        ]
        g11 = g1[:, :128]
        folded = jnp.where((row > col)[:64] & (col < 64)[:64], pltpu.roll(g2[64:], 64, 1), g2[:64])
        lines = jnp.where(row[:64] == 0, diagonal(g11), jnp.where(row[:64] == 1, diagonal(g2), 0.0))
        dst[0:128, :] = jnp.where(row <= col, g0[:, :128], g11).astype(dst.dtype)
        dst[128:256, :] = g0[:, 128:256].astype(dst.dtype)
        dst[256:384, :] = g0[:, 256:].astype(dst.dtype)
        dst[384:512, :] = g1[:, 128:].astype(dst.dtype)
        dst[512:576, :] = folded.astype(dst.dtype)
        dst[576:640, :] = lines.astype(dst.dtype)

    def gram_of(own_layer, t, dst):
        loads[own_layer, t].wait()
        layer = c if own_layer else other
        gram(grd[layer] if t == 4 else hid[layer, :, t * BLK : (t + 1) * BLK], dst.at[t])

    started, from_sibling, from_y, from_z = [], {}, {}, {}

    def to_sibling(t):
        copy = send(abuf.at[t], arec.at[t], a_s.at[t], a_r.at[t], dev(c=other))
        copy.start()
        started.append(copy)
        from_sibling[t] = copy

    def to_quarters(t):
        from_sibling[t].wait_recv()
        total = own[t] + arec[t].astype(F32)
        own[t] = total
        s1[t] = total.astype(BF16)
        for by in (2, 1, 3):
            to = turn(y, by)
            copy = send(s1.at[t, part(to)], brec.at[by - 1, t], b_s.at[t, by - 1], b_r.at[t, by - 1], dev(y=to))
            copy.start()
            started.append(copy)
            from_y[t, by] = copy

    for n, t in enumerate(ORDER):
        gram_of(0, t, abuf)
        if n == 0:
            pl.semaphore_wait(barrier, jnp.where(y == y_goal, 15, 16))
        to_sibling(t)
        gram_of(1, t, own)
        if n:
            to_quarters(ORDER[n - 1])
    to_quarters(ORDER[-1])

    def sum_y(t):
        for by in (1, 2, 3):
            from_y[t, by].wait_recv()
        total = own[t, part(y)]
        for by in (1, 2, 3):
            total += brec[by - 1, t].astype(F32)
        ysum[t] = total
        cs[t] = total.astype(BF16)

    def to_users(t):
        sum_y(t)
        goal = 2 * lax.rem(x, 2) + t // 2

        @pl.when(z != goal)
        def _():
            slot = lax.rem(z - goal + 4, 4) - 1
            send(cs.at[t], crec.at[slot, t % 2], c_s.at[t], c_r.at[slot, t % 2], dev(z=goal)).start()

    def spread(e):
        for by in (2, 1, 3, 0):
            copy = send(
                dtot.at[e], ft.at[c, part(y)], e_s.at[e, by], e_r.at[c, y], dev(y=y_goal, c=e, x=turn(x, by))
            )
            if by:
                copy.start()
            else:
                here = (y_goal == y) & (c == e)

                @pl.when(here)
                def _():
                    ft[c, part(y)] = dtot[e]

                @pl.when(jnp.logical_not(here))
                def _():
                    copy.start()

    def cross(e):
        return send(dtot.at[e], dtot.at[e], d_s.at[e], d_r.at[e], dev(zh=1 - zh, x=x_pair))

    def from_users(e):
        @pl.when(active)
        def _():
            for by in (1, 2, 3):
                send(cs.at[0], crec.at[by - 1, e], c_s.at[0], c_r.at[by - 1, e], dev(c=other)).wait_recv()
            total = ysum[2 * lax.rem(z, 2) + e]
            for by in (1, 2, 3):
                total += crec[by - 1, e].astype(F32)
            dtot[e] = total.astype(BF16)
            cross(e).start()
            spread(e)

    def from_cross(e):
        @pl.when(jnp.logical_not(active))
        def _():
            cross(e).wait_recv()
            spread(e)

    def to_every_z():
        sum_y(4)
        for by in (1, 2, 3):
            copy = send(cs.at[4], grec.at[by - 1], g_s.at[by - 1], g_r.at[by - 1], dev(z=turn(z, by)))
            copy.start()
            started.append(copy)
            from_z[by] = copy

    def gather_gradient_tile():
        for by in (1, 2, 3):
            from_z[by].wait_recv()
        total = ysum[4]
        for by in (1, 2, 3):
            total += grec[by - 1].astype(F32)
        gtot[...] = total.astype(BF16)
        ft[2, part(y)] = gtot[...]
        for by in (1, 2, 3):
            copy = send(gtot, ft.at[2, part(y)], h_s.at[by - 1], h_r.at[by - 1], dev(y=turn(y, by)))
            copy.start()
            started.append(copy)

    to_users(0)
    to_users(2)
    to_every_z()
    from_users(0)
    to_users(1)
    to_users(3)
    from_cross(0)
    gather_gradient_tile()
    from_users(1)
    from_cross(1)

    eye = jnp.where(
        lax.broadcasted_iota(jnp.int32, (BLK, BLK), 0) == lax.broadcasted_iota(jnp.int32, (BLK, BLK), 1), 1.0, 0.0
    )

    def put(slot, value, column):
        high = value.astype(BF16)
        low = (value - high.astype(F32)).astype(BF16)
        span = slice(column * BLK, (column + 1) * BLK)
        rhs[slot, 0:BLK, span] = high
        rhs[slot, BLK : 2 * BLK, span] = low
        rhs[slot, 2 * BLK :, span] = high
        if column == 0:
            lhs[slot, :, 0:BLK] = high
            lhs[slot, :, BLK : 2 * BLK] = high
            lhs[slot, :, 2 * BLK :] = low

    def dot(a, b):
        return jnp.dot(a, b, preferred_element_type=F32)

    def inverses(slots):
        scale = {}
        for s in slots:
            def rows(first, count):
                return ft[s, first : first + count].astype(F32)

            mixed, turned = rows(0, 128), rows(0, 128).T
            folded = rows(512, 64)
            lines = rows(576, 16)
            square = jnp.concatenate([folded, pltpu.roll(folded, 64, 1)], axis=0)
            upright = ((row < 64) & (row <= col)) | ((row >= 64) & (col >= 64) & (row > col))
            block = {
                (0, 0): jnp.where(row <= col, mixed, turned),
                (0, 1): rows(128, 128),
                (0, 2): rows(256, 128),
                (1, 1): jnp.where(row == col, lines[0:1], jnp.where(row > col, mixed, turned)),
                (1, 2): rows(384, 128),
                (2, 2): jnp.where((row == col) & (row >= 64), lines[1:2], jnp.where(upright, square, square.T)),
            }
            for r in range(3):
                for k in range(3):
                    tile = block[r, k] if r <= k else block[k, r].T
                    acc[s, r * 128 : (r + 1) * 128, k * 128 : (k + 1) * 128] = tile
        for s in slots:
            factor = acc[s] * (1.0 / 8192.0) + DAMPING * eye
            bound = jnp.max(jnp.sum(jnp.abs(factor), axis=1, keepdims=True), axis=0, keepdims=True)
            scale[s] = 1.0 / bound
            residue = eye - factor * scale[s]
            acc[s] = eye + residue
            put(s, residue, 0)
            put(s, acc[s], 1)
        for s in slots:
            put(s, dot(lhs[s], rhs[s, :, :BLK]), 0)
        for _ in range(2):
            for s in slots:
                both = dot(lhs[s], rhs[s])
                acc[s] += both[:, BLK:]
                put(s, both[:, :BLK], 0)
                put(s, acc[s], 1)
        for s in slots:
            acc[s] += dot(lhs[s], rhs[s, :, BLK:])
            square = dot(lhs[s, :, :BLK], rhs[s, :BLK, :BLK]).astype(BF16)
            acc[s] += dot(square, acc[s].astype(BF16))
        return [(acc[s] * scale[s]).astype(BF16) for s in slots]

    for by in (1, 2, 3):
        send(gtot, ft.at[2, part(y)], h_s.at[by - 1], h_r.at[by - 1], dev(y=turn(y, by))).wait_recv()
    ginv[c] = inverses((2,))[0]
    swap = send(ginv.at[c], ginv.at[c], i_s, i_r, dev(c=other))
    swap.start()
    load_w.wait()
    for layer in (0, 1):
        for yy in range(4):
            mine = (x == x_from) & (c == layer) & (y == yy)

            @pl.when(jnp.logical_not(mine))
            def _():
                send(
                    dtot.at[0], ft.at[layer, part(yy)], e_s.at[0, 0], e_r.at[layer, yy], dev(c=other)
                ).wait_recv()
    for layer, inverse in enumerate(inverses((0, 1))):
        left[layer] = dot(inverse, wv[layer]).astype(BF16)
    swap.wait()
    for layer in (0, 1):
        out[layer] = dot(left[layer], ginv[layer]).astype(BF16)

    for copy in started:
        copy.wait_send()
    for t in range(4):
        @pl.when(z != 2 * lax.rem(x, 2) + t // 2)
        def _():
            send(cs.at[0], crec.at[0, 0], c_s.at[t], c_r.at[0, 0], dev(c=other)).wait_send()

    @pl.when(active)
    def _():
        for e in (0, 1):
            cross(e).wait_send()

    for e in (0, 1):
        for by in range(4):
            copy = send(dtot.at[0], ft.at[0, part(0)], e_s.at[e, by], e_r.at[0, 0], dev(c=other))
            if by:
                copy.wait_send()
            else:
                @pl.when((y_goal != y) | (c != e))
                def _():
                    copy.wait_send()


def shards(hidden_acts, out_grads, token_picks, weight_grads):
    dma = pltpu.SemaphoreType.DMA
    vmem = pltpu.VMEM
    return pl.pallas_call(
        kernel,
        out_shape=jax.ShapeDtypeStruct(weight_grads.shape, BF16),
        in_specs=[
            pl.BlockSpec(memory_space=pl.ANY),
            pl.BlockSpec(memory_space=pl.ANY),
            pl.BlockSpec(memory_space=vmem),
            pl.BlockSpec(memory_space=pl.ANY),
        ],
        out_specs=pl.BlockSpec(memory_space=vmem),
        scratch_shapes=[
            vmem(hidden_acts.shape, BF16), vmem(out_grads.shape, BF16), vmem(weight_grads.shape, BF16),
            vmem((POOL, BLK), BF16),
            vmem((5, ROWS, 128), BF16), vmem((5, ROWS, 128), BF16), vmem((5, ROWS, 128), F32), vmem((5, ROWS, 128), BF16),
            vmem((3, 5, PART, 128), BF16), vmem((5, PART, 128), F32), vmem((5, PART, 128), BF16),
            vmem((3, 2, PART, 128), BF16), vmem((3, PART, 128), BF16), vmem((2, PART, 128), BF16),
            vmem((PART, 128), BF16), vmem((3, ROWS, 128), BF16),
            vmem((3, BLK, 3 * BLK), BF16), vmem((3, 3 * BLK, 2 * BLK), BF16), vmem((3, BLK, BLK), F32),
            vmem((2, BLK, BLK), BF16), vmem((2, BLK, BLK), BF16),
            dma((11,)), dma((5,)), dma((5,)), dma((5, 3)), dma((5, 3)), dma((4,)), dma((3, 2)), dma((3,)), dma((3,)),
            dma((2,)), dma((2,)), dma((2, 4)), dma((2, 4)), dma((3,)), dma((3,)), dma, dma,
        ],
        compiler_params=pltpu.CompilerParams(
            collective_id=0, has_side_effects=True, vmem_limit_bytes=53 * 2**20
        ),
    )(hidden_acts, out_grads, token_picks, weight_grads)


def solution(mesh):
    placed = (P(None, "dp", "mp"), P(None, "dp", "mp"), P("dp", None), P(None, "dp", "mp"))
    return jax.shard_map(shards, mesh=mesh, in_specs=placed, out_specs=P(None, "dp", "mp"), check_vma=False)
```

```python
import jax
import jax.numpy as jnp
from jax import lax
from jax.experimental import pallas as pl
from jax.experimental.pallas import tpu as pltpu
from jax.sharding import PartitionSpec as P

BLK = 384
SAMPLE = 256
POOL = 512
ROWS = 640
PART = 160
SLICE = 48
DAMPING = 0.1
MESH = pl.DeviceIdType.MESH
F32 = jnp.float32
BF16 = jnp.bfloat16
ORDER = (0, 2, 4, 1, 3)


def kernel(
    hid_hbm, grd_hbm, picks, w_hbm, out,
    hid, grd, wv, mask, abuf, arec, own, s1, brec, ysum, cs, crec, grec, dtot, gtot, gsum, gpart, gz, ft, lhs, rhs, acc, ginv, left,
    load_sem, a_s, a_r, b_s, b_r, c_s, c_r, g_s, g_r, k_s, k_r, d_s, d_r, e_s, e_r, h_s, h_r, i_s, i_r,
):
    i, m = lax.axis_index("dp"), lax.axis_index("mp")
    c, z, y = lax.rem(i, 2), lax.rem(i // 2, 4), i // 8
    zh, x = m // 4, lax.rem(m, 4)
    active = z // 2 == lax.rem(x, 2)
    x_pair = x + 1 - 2 * lax.rem(x, 2)
    x_src = lax.rem(y, 2) * 2 + z // 2
    x_from = jnp.where(zh == y // 2, x_src, x_src + 1 - 2 * lax.rem(x_src, 2))
    y_goal = jnp.where(active, zh, 1 - zh) * 2 + x // 2

    def dev(y=y, z=z, c=c, zh=zh, x=x):
        return ((y * 4 + z) * 2 + c, zh * 4 + x)

    def turn(v, by):
        return lax.rem(v + by, 4)

    def send(src, dst, ss, rs, to):
        return pltpu.make_async_remote_copy(
            src_ref=src, dst_ref=dst, send_sem=ss, recv_sem=rs, device_id=to, device_id_type=MESH
        )

    def part(q):
        return pl.ds(pl.multiple_of(q * PART, PART), PART)

    other = 1 - c
    loads = {}
    for n, (t, own_layer) in enumerate([(t, own_layer) for t in ORDER for own_layer in (0, 1)]):
        layer = c if own_layer else other
        if t == 4:
            copy = pltpu.make_async_copy(grd_hbm.at[layer], grd.at[layer], load_sem.at[n])
        else:
            span = pl.ds(t * BLK, BLK)
            copy = pltpu.make_async_copy(hid_hbm.at[layer, :, span], hid.at[layer, :, span], load_sem.at[n])
        copy.start()
        loads[own_layer, t] = copy
    load_w = pltpu.make_async_copy(w_hbm, wv, load_sem.at[10])
    load_w.start()

    barrier = pltpu.get_barrier_semaphore()

    def greet(to):
        pl.semaphore_signal(barrier, inc=1, device_id=to, device_id_type=MESH)

    greet(dev(c=1 - c))
    greet(dev(zh=1 - zh, x=x_pair))
    for by in (1, 2, 3):
        greet(dev(y=turn(y, by)))
        greet(dev(z=turn(z, by)))
    for cc in (0, 1):
        for by in range(4):
            if by:
                greet(dev(x=x_from, y=turn(y, by), c=cc))
            else:
                @pl.when((x_from != x) | (c != cc))
                def _():
                    greet(dev(x=x_from, c=cc))

    token = lax.broadcasted_iota(jnp.int32, (POOL, SAMPLE), 0)
    hit = jnp.where(token == picks[:, :SAMPLE], 1.0, 0.0)
    mask[...] = jnp.broadcast_to(jnp.max(hit, axis=1, keepdims=True), (POOL, BLK)).astype(BF16)

    row = lax.broadcasted_iota(jnp.int32, (128, 128), 0)
    col = lax.broadcasted_iota(jnp.int32, (128, 128), 1)

    def diagonal(block):
        return jnp.sum(jnp.where(row == col, block, 0.0), axis=0, keepdims=True)

    def gram(tile, dst):
        masked = tile * mask[...]
        g0, g1, g2 = [
            lax.dot_general(
                masked[:, r * 128 : (r + 1) * 128], tile[:, r * 128 :], (((0,), (0,)), ((), ())),
                preferred_element_type=F32,
            )
            for r in range(3)
        ]
        g11 = g1[:, :128]
        folded = jnp.where((row > col)[:64] & (col < 64)[:64], pltpu.roll(g2[64:], 64, 1), g2[:64])
        lines = jnp.where(row[:64] == 0, diagonal(g11), jnp.where(row[:64] == 1, diagonal(g2), 0.0))
        dst[0:128, :] = jnp.where(row <= col, g0[:, :128], g11).astype(dst.dtype)
        dst[128:256, :] = g0[:, 128:256].astype(dst.dtype)
        dst[256:384, :] = g0[:, 256:].astype(dst.dtype)
        dst[384:512, :] = g1[:, 128:].astype(dst.dtype)
        dst[512:576, :] = folded.astype(dst.dtype)
        dst[576:640, :] = lines.astype(dst.dtype)

    def gram_of(own_layer, t, dst):
        loads[own_layer, t].wait()
        layer = c if own_layer else other
        gram(grd[layer] if t == 4 else hid[layer, :, t * BLK : (t + 1) * BLK], dst.at[t])

    started, from_sibling, from_y, from_z = [], {}, {}, {}

    def to_sibling(t):
        copy = send(abuf.at[t], arec.at[t], a_s.at[t], a_r.at[t], dev(c=other))
        copy.start()
        started.append(copy)
        from_sibling[t] = copy

    def to_quarters(t):
        from_sibling[t].wait_recv()
        total = own[t] + arec[t].astype(F32)
        own[t] = total
        s1[t] = total.astype(BF16)
        for by in (2, 1, 3):
            to = turn(y, by)
            copy = send(s1.at[t, part(to)], brec.at[by - 1, t], b_s.at[t, by - 1], b_r.at[t, by - 1], dev(y=to))
            copy.start()
            started.append(copy)
            from_y[t, by] = copy

    for n, t in enumerate(ORDER):
        gram_of(0, t, abuf)
        if n == 0:
            pl.semaphore_wait(barrier, jnp.where(y == y_goal, 15, 16))
        to_sibling(t)
        gram_of(1, t, own)
        if n:
            to_quarters(ORDER[n - 1])
    to_quarters(ORDER[-1])

    def sum_y(t):
        for by in (1, 2, 3):
            from_y[t, by].wait_recv()
        total = own[t, part(y)]
        for by in (1, 2, 3):
            total += brec[by - 1, t].astype(F32)
        ysum[t] = total
        cs[t] = total.astype(BF16)

    def to_users(t):
        sum_y(t)
        goal = 2 * lax.rem(x, 2) + t // 2

        @pl.when(z != goal)
        def _():
            slot = lax.rem(z - goal + 4, 4) - 1
            send(cs.at[t], crec.at[slot, t % 2], c_s.at[t], c_r.at[slot, t % 2], dev(z=goal)).start()

    def rows_of(q):
        return pl.ds(pl.multiple_of(q * SLICE, SLICE), SLICE)

    def to_slices():
        sum_y(4)
        gsum[0:PART] = ysum[4]
        gpart[0:PART] = cs[4]
        gsum[PART:] = jnp.zeros((4 * SLICE - PART, 128), F32)
        gpart[PART:] = jnp.zeros((4 * SLICE - PART, 128), BF16)
        for by in (1, 2, 3):
            to = turn(z, by)
            copy = send(gpart.at[rows_of(to)], grec.at[by - 1], g_s.at[by - 1], g_r.at[by - 1], dev(z=to))
            copy.start()
            started.append(copy)
            from_z[by] = copy

    def gather_slices():
        for by in (1, 2, 3):
            from_z[by].wait_recv()
        total = gsum[rows_of(z)]
        for by in (1, 2, 3):
            total += grec[by - 1].astype(F32)
        gtot[...] = total.astype(BF16)
        gz[rows_of(z)] = gtot[...]
        for by in (1, 2, 3):
            copy = send(gtot, gz.at[rows_of(z)], k_s.at[by - 1], k_r.at[by - 1], dev(z=turn(z, by)))
            copy.start()
            started.append(copy)

    def gather_gradient_tile():
        for by in (1, 2, 3):
            send(gtot, gz.at[rows_of(z)], k_s.at[by - 1], k_r.at[by - 1], dev(z=turn(z, by))).wait_recv()
        ft[2, part(y)] = gz[0:PART]
        for by in (1, 2, 3):
            copy = send(gz.at[0:PART], ft.at[2, part(y)], h_s.at[by - 1], h_r.at[by - 1], dev(y=turn(y, by)))
            copy.start()
            started.append(copy)

    def spread(e):
        for by in (2, 1, 3, 0):
            copy = send(
                dtot.at[e], ft.at[c, part(y)], e_s.at[e, by], e_r.at[c, y], dev(y=y_goal, c=e, x=turn(x, by))
            )
            if by:
                copy.start()
            else:
                here = (y_goal == y) & (c == e)

                @pl.when(here)
                def _():
                    ft[c, part(y)] = dtot[e]

                @pl.when(jnp.logical_not(here))
                def _():
                    copy.start()

    def cross(e):
        return send(dtot.at[e], dtot.at[e], d_s.at[e], d_r.at[e], dev(zh=1 - zh, x=x_pair))

    def from_users(e):
        @pl.when(active)
        def _():
            for by in (1, 2, 3):
                send(cs.at[0], crec.at[by - 1, e], c_s.at[0], c_r.at[by - 1, e], dev(c=other)).wait_recv()
            total = ysum[2 * lax.rem(z, 2) + e]
            for by in (1, 2, 3):
                total += crec[by - 1, e].astype(F32)
            dtot[e] = total.astype(BF16)
            cross(e).start()
            spread(e)

    def from_cross(e):
        @pl.when(jnp.logical_not(active))
        def _():
            cross(e).wait_recv()
            spread(e)

    to_users(0)
    to_users(2)
    to_slices()
    from_users(0)
    to_users(1)
    gather_slices()
    to_users(3)
    from_cross(0)
    gather_gradient_tile()
    from_users(1)
    from_cross(1)

    eye = jnp.where(
        lax.broadcasted_iota(jnp.int32, (BLK, BLK), 0) == lax.broadcasted_iota(jnp.int32, (BLK, BLK), 1), 1.0, 0.0
    )

    def put(slot, value, column):
        high = value.astype(BF16)
        low = (value - high.astype(F32)).astype(BF16)
        span = slice(column * BLK, (column + 1) * BLK)
        rhs[slot, 0:BLK, span] = high
        rhs[slot, BLK : 2 * BLK, span] = high
        rhs[slot, 2 * BLK :, span] = low
        if column == 0:
            lhs[slot, :, 0:BLK] = high
            lhs[slot, :, BLK : 2 * BLK] = low
            lhs[slot, :, 2 * BLK :] = high

    def dot(a, b):
        return jnp.dot(a, b, preferred_element_type=F32)

    def inverses(slots):
        scale = {}
        for s in slots:
            def rows(first, count):
                return ft[s, first : first + count].astype(F32)

            mixed, turned = rows(0, 128), rows(0, 128).T
            folded = rows(512, 64)
            lines = rows(576, 16)
            square = jnp.concatenate([folded, pltpu.roll(folded, 64, 1)], axis=0)
            upright = ((row < 64) & (row <= col)) | ((row >= 64) & (col >= 64) & (row > col))
            block = {
                (0, 0): jnp.where(row <= col, mixed, turned),
                (0, 1): rows(128, 128),
                (0, 2): rows(256, 128),
                (1, 1): jnp.where(row == col, lines[0:1], jnp.where(row > col, mixed, turned)),
                (1, 2): rows(384, 128),
                (2, 2): jnp.where((row == col) & (row >= 64), lines[1:2], jnp.where(upright, square, square.T)),
            }
            for r in range(3):
                for k in range(3):
                    tile = block[r, k] if r <= k else block[k, r].T
                    acc[s, r * 128 : (r + 1) * 128, k * 128 : (k + 1) * 128] = tile
        for s in slots:
            factor = acc[s] * (1.0 / 8192.0) + DAMPING * eye
            bound = jnp.max(jnp.sum(jnp.abs(factor), axis=1, keepdims=True), axis=0, keepdims=True)
            scale[s] = 1.0 / bound
            residue = eye - factor * scale[s]
            acc[s] = eye + residue
            put(s, residue, 0)
            put(s, acc[s], 1)
        for s in slots:
            put(s, dot(lhs[s], rhs[s, :, :BLK]), 0)
        for _ in range(2):
            for s in slots:
                both = dot(lhs[s], rhs[s])
                acc[s] += both[:, BLK:]
                put(s, both[:, :BLK], 0)
                put(s, acc[s], 1)
        for s in slots:
            acc[s] += dot(lhs[s, :, : 2 * BLK], rhs[s, : 2 * BLK, BLK:])
            square = dot(lhs[s, :, :BLK], rhs[s, :BLK, :BLK]).astype(BF16)
            acc[s] += dot(square, acc[s].astype(BF16))
        return [(acc[s] * scale[s]).astype(BF16) for s in slots]

    for by in (1, 2, 3):
        send(gz.at[0:PART], ft.at[2, part(y)], h_s.at[by - 1], h_r.at[by - 1], dev(y=turn(y, by))).wait_recv()
    ginv[c] = inverses((2,))[0]
    swap = send(ginv.at[c], ginv.at[c], i_s, i_r, dev(c=other))
    swap.start()
    load_w.wait()
    for layer in (0, 1):
        for yy in range(4):
            mine = (x == x_from) & (c == layer) & (y == yy)

            @pl.when(jnp.logical_not(mine))
            def _():
                send(
                    dtot.at[0], ft.at[layer, part(yy)], e_s.at[0, 0], e_r.at[layer, yy], dev(c=other)
                ).wait_recv()
    for layer, inverse in enumerate(inverses((0, 1))):
        left[layer] = dot(inverse, wv[layer]).astype(BF16)
    swap.wait()
    for layer in (0, 1):
        out[layer] = dot(left[layer], ginv[layer]).astype(BF16)

    for copy in started:
        copy.wait_send()
    for t in range(4):
        @pl.when(z != 2 * lax.rem(x, 2) + t // 2)
        def _():
            send(cs.at[0], crec.at[0, 0], c_s.at[t], c_r.at[0, 0], dev(c=other)).wait_send()

    @pl.when(active)
    def _():
        for e in (0, 1):
            cross(e).wait_send()

    for e in (0, 1):
        for by in range(4):
            copy = send(dtot.at[0], ft.at[0, part(0)], e_s.at[e, by], e_r.at[0, 0], dev(c=other))
            if by:
                copy.wait_send()
            else:
                @pl.when((y_goal != y) | (c != e))
                def _():
                    copy.wait_send()


def shards(hidden_acts, out_grads, token_picks, weight_grads):
    dma = pltpu.SemaphoreType.DMA
    vmem = pltpu.VMEM
    return pl.pallas_call(
        kernel,
        out_shape=jax.ShapeDtypeStruct(weight_grads.shape, BF16),
        in_specs=[
            pl.BlockSpec(memory_space=pl.ANY),
            pl.BlockSpec(memory_space=pl.ANY),
            pl.BlockSpec(memory_space=vmem),
            pl.BlockSpec(memory_space=pl.ANY),
        ],
        out_specs=pl.BlockSpec(memory_space=vmem),
        scratch_shapes=[
            vmem(hidden_acts.shape, BF16), vmem(out_grads.shape, BF16), vmem(weight_grads.shape, BF16),
            vmem((POOL, BLK), BF16),
            vmem((5, ROWS, 128), BF16), vmem((5, ROWS, 128), BF16), vmem((5, ROWS, 128), F32), vmem((5, ROWS, 128), BF16),
            vmem((3, 5, PART, 128), BF16), vmem((5, PART, 128), F32), vmem((5, PART, 128), BF16),
            vmem((3, 2, PART, 128), BF16), vmem((3, SLICE, 128), BF16), vmem((2, PART, 128), BF16),
            vmem((SLICE, 128), BF16), vmem((4 * SLICE, 128), F32), vmem((4 * SLICE, 128), BF16), vmem((4 * SLICE, 128), BF16),
            vmem((3, ROWS, 128), BF16),
            vmem((3, BLK, 3 * BLK), BF16), vmem((3, 3 * BLK, 2 * BLK), BF16), vmem((3, BLK, BLK), F32),
            vmem((2, BLK, BLK), BF16), vmem((2, BLK, BLK), BF16),
            dma((11,)), dma((5,)), dma((5,)), dma((5, 3)), dma((5, 3)), dma((4,)), dma((3, 2)), dma((3,)), dma((3,)), dma((3,)), dma((3,)),
            dma((2,)), dma((2,)), dma((2, 4)), dma((2, 4)), dma((3,)), dma((3,)), dma, dma,
        ],
        compiler_params=pltpu.CompilerParams(
            collective_id=0, has_side_effects=True, vmem_limit_bytes=53 * 2**20
        ),
    )(hidden_acts, out_grads, token_picks, weight_grads)


def solution(mesh):
    placed = (P(None, "dp", "mp"), P(None, "dp", "mp"), P("dp", None), P(None, "dp", "mp"))
    return jax.shard_map(shards, mesh=mesh, in_specs=placed, out_specs=P(None, "dp", "mp"), check_vma=False)
```

```python
import jax
import jax.numpy as jnp
from jax import lax
from jax.experimental import pallas as pl
from jax.experimental.pallas import tpu as pltpu
from jax.sharding import PartitionSpec as P

BLK = 384
SAMPLE = 256
POOL = 512
ROWS = 640
PART = 160
SLICE = 48
DAMPING = 0.1
MESH = pl.DeviceIdType.MESH
F32 = jnp.float32
BF16 = jnp.bfloat16
ORDER = (0, 2, 4, 1, 3)


def kernel(
    hid_hbm, grd_hbm, picks, w_hbm, out,
    hid, grd, wv, mask, abuf, arec, own, s1, brec, ysum, cs, crec, grec, dtot, gtot, gsum, gpart, gz, ft, lhs, rhs, acc, ginv, left,
    load_sem, a_s, a_r, b_s, b_r, c_s, c_r, g_s, g_r, k_s, k_r, d_s, d_r, e_s, e_r, h_s, h_r, i_s, i_r,
):
    i, m = lax.axis_index("dp"), lax.axis_index("mp")
    c, z, y = lax.rem(i, 2), lax.rem(i // 2, 4), i // 8
    zh, x = m // 4, lax.rem(m, 4)
    active = z // 2 == lax.rem(x, 2)
    x_pair = x + 1 - 2 * lax.rem(x, 2)
    x_src = lax.rem(y, 2) * 2 + z // 2
    x_from = jnp.where(zh == y // 2, x_src, x_src + 1 - 2 * lax.rem(x_src, 2))
    y_goal = jnp.where(active, zh, 1 - zh) * 2 + x // 2

    def dev(y=y, z=z, c=c, zh=zh, x=x):
        return ((y * 4 + z) * 2 + c, zh * 4 + x)

    def turn(v, by):
        return lax.rem(v + by, 4)

    def send(src, dst, ss, rs, to):
        return pltpu.make_async_remote_copy(
            src_ref=src, dst_ref=dst, send_sem=ss, recv_sem=rs, device_id=to, device_id_type=MESH
        )

    def part(q):
        return pl.ds(pl.multiple_of(q * PART, PART), PART)

    other = 1 - c
    loads = {}
    for n, (t, own_layer) in enumerate([(t, own_layer) for t in ORDER for own_layer in (0, 1)]):
        layer = c if own_layer else other
        if t == 4:
            copy = pltpu.make_async_copy(grd_hbm.at[layer], grd.at[layer], load_sem.at[n])
        else:
            span = pl.ds(t * BLK, BLK)
            copy = pltpu.make_async_copy(hid_hbm.at[layer, :, span], hid.at[layer, :, span], load_sem.at[n])
        loads[own_layer, t] = copy
        if n < 2:
            copy.start()

    barrier = pltpu.get_barrier_semaphore()

    def greet(to):
        pl.semaphore_signal(barrier, inc=1, device_id=to, device_id_type=MESH)

    greet(dev(zh=1 - zh, x=x_pair))
    for cc in (0, 1):
        for by in range(4):
            if by:
                greet(dev(x=x_from, y=turn(y, by), c=cc))
            else:
                @pl.when((x_from != x) | (c != cc))
                def _():
                    greet(dev(x=x_from, c=cc))

    for by in (1, 2, 3):
        greet(dev(y=turn(y, by)))
        greet(dev(z=turn(z, by)))
    greet(dev(c=1 - c))

    for copy in list(loads.values())[2:]:
        copy.start()
    load_w = pltpu.make_async_copy(w_hbm, wv, load_sem.at[10])
    load_w.start()

    token = lax.broadcasted_iota(jnp.int32, (POOL, SAMPLE), 0)
    hit = jnp.where(token == picks[:, :SAMPLE], 1.0, 0.0)
    mask[...] = jnp.broadcast_to(jnp.max(hit, axis=1, keepdims=True), (POOL, BLK)).astype(BF16)

    row = lax.broadcasted_iota(jnp.int32, (128, 128), 0)
    col = lax.broadcasted_iota(jnp.int32, (128, 128), 1)

    def diagonal(block):
        return jnp.sum(jnp.where(row == col, block, 0.0), axis=0, keepdims=True)

    def gram(tile, dst):
        masked = tile * mask[...]
        g0, g1, g2 = [
            lax.dot_general(
                masked[:, r * 128 : (r + 1) * 128], tile[:, r * 128 :], (((0,), (0,)), ((), ())),
                preferred_element_type=F32,
            )
            for r in range(3)
        ]
        g11 = g1[:, :128]
        folded = jnp.where((row > col)[:64] & (col < 64)[:64], pltpu.roll(g2[64:], 64, 1), g2[:64])
        lines = jnp.where(row[:64] == 0, diagonal(g11), jnp.where(row[:64] == 1, diagonal(g2), 0.0))
        dst[0:128, :] = jnp.where(row <= col, g0[:, :128], g11).astype(dst.dtype)
        dst[128:256, :] = g0[:, 128:256].astype(dst.dtype)
        dst[256:384, :] = g0[:, 256:].astype(dst.dtype)
        dst[384:512, :] = g1[:, 128:].astype(dst.dtype)
        dst[512:576, :] = folded.astype(dst.dtype)
        dst[576:640, :] = lines.astype(dst.dtype)

    def gram_of(own_layer, t, dst):
        loads[own_layer, t].wait()
        layer = c if own_layer else other
        gram(grd[layer] if t == 4 else hid[layer, :, t * BLK : (t + 1) * BLK], dst.at[t])

    started, from_sibling, from_y, from_z = [], {}, {}, {}

    def to_sibling(t):
        copy = send(abuf.at[t], arec.at[t], a_s.at[t], a_r.at[t], dev(c=other))
        copy.start()
        started.append(copy)
        from_sibling[t] = copy

    def to_quarters(t):
        from_sibling[t].wait_recv()
        total = own[t] + arec[t].astype(F32)
        own[t] = total
        s1[t] = total.astype(BF16)
        for by in (2, 1, 3):
            to = turn(y, by)
            copy = send(s1.at[t, part(to)], brec.at[by - 1, t], b_s.at[t, by - 1], b_r.at[t, by - 1], dev(y=to))
            copy.start()
            started.append(copy)
            from_y[t, by] = copy

    for n, t in enumerate(ORDER):
        if n == 0:
            gram_of(0, t, abuf)
            pl.semaphore_wait(barrier, jnp.where(y == y_goal, 15, 16))
            to_sibling(t)
        if n + 1 < len(ORDER):
            gram_of(0, ORDER[n + 1], abuf)
            to_sibling(ORDER[n + 1])
        gram_of(1, t, own)
        to_quarters(t)

    def sum_y(t):
        for by in (1, 2, 3):
            from_y[t, by].wait_recv()
        total = own[t, part(y)]
        for by in (1, 2, 3):
            total += brec[by - 1, t].astype(F32)
        ysum[t] = total
        cs[t] = total.astype(BF16)

    def to_users(t):
        sum_y(t)
        goal = 2 * lax.rem(x, 2) + t // 2

        @pl.when(z != goal)
        def _():
            slot = lax.rem(z - goal + 4, 4) - 1
            send(cs.at[t], crec.at[slot, t % 2], c_s.at[t], c_r.at[slot, t % 2], dev(z=goal)).start()

    def rows_of(q):
        return pl.ds(pl.multiple_of(q * SLICE, SLICE), SLICE)

    def to_slices():
        sum_y(4)
        gsum[0:PART] = ysum[4]
        gpart[0:PART] = cs[4]
        gsum[PART:] = jnp.zeros((4 * SLICE - PART, 128), F32)
        gpart[PART:] = jnp.zeros((4 * SLICE - PART, 128), BF16)
        for by in (1, 2, 3):
            to = turn(z, by)
            copy = send(gpart.at[rows_of(to)], grec.at[by - 1], g_s.at[by - 1], g_r.at[by - 1], dev(z=to))
            copy.start()
            started.append(copy)
            from_z[by] = copy

    def gather_slices():
        for by in (1, 2, 3):
            from_z[by].wait_recv()
        total = gsum[rows_of(z)]
        for by in (1, 2, 3):
            total += grec[by - 1].astype(F32)
        gtot[...] = total.astype(BF16)
        gz[rows_of(z)] = gtot[...]
        for by in (1, 2, 3):
            copy = send(gtot, gz.at[rows_of(z)], k_s.at[by - 1], k_r.at[by - 1], dev(z=turn(z, by)))
            copy.start()
            started.append(copy)

    def gather_gradient_tile():
        for by in (1, 2, 3):
            send(gtot, gz.at[rows_of(z)], k_s.at[by - 1], k_r.at[by - 1], dev(z=turn(z, by))).wait_recv()
        ft[2, part(y)] = gz[0:PART]
        for by in (1, 2, 3):
            copy = send(gz.at[0:PART], ft.at[2, part(y)], h_s.at[by - 1], h_r.at[by - 1], dev(y=turn(y, by)))
            copy.start()
            started.append(copy)

    def spread(e):
        for by in (2, 1, 3, 0):
            copy = send(
                dtot.at[e], ft.at[c, part(y)], e_s.at[e, by], e_r.at[c, y], dev(y=y_goal, c=e, x=turn(x, by))
            )
            if by:
                copy.start()
            else:
                here = (y_goal == y) & (c == e)

                @pl.when(here)
                def _():
                    ft[c, part(y)] = dtot[e]

                @pl.when(jnp.logical_not(here))
                def _():
                    copy.start()

    def cross(e):
        return send(dtot.at[e], dtot.at[e], d_s.at[e], d_r.at[e], dev(zh=1 - zh, x=x_pair))

    def from_users(e):
        @pl.when(active)
        def _():
            for by in (1, 2, 3):
                send(cs.at[0], crec.at[by - 1, e], c_s.at[0], c_r.at[by - 1, e], dev(c=other)).wait_recv()
            total = ysum[2 * lax.rem(z, 2) + e]
            for by in (1, 2, 3):
                total += crec[by - 1, e].astype(F32)
            dtot[e] = total.astype(BF16)
            cross(e).start()
            spread(e)

    def from_cross(e):
        @pl.when(jnp.logical_not(active))
        def _():
            cross(e).wait_recv()
            spread(e)

    to_users(0)
    to_users(2)
    to_slices()
    from_users(0)
    to_users(1)
    gather_slices()
    to_users(3)
    from_cross(0)
    gather_gradient_tile()
    from_users(1)
    from_cross(1)

    eye = jnp.where(
        lax.broadcasted_iota(jnp.int32, (BLK, BLK), 0) == lax.broadcasted_iota(jnp.int32, (BLK, BLK), 1), 1.0, 0.0
    )

    def put(slot, value, column):
        high = value.astype(BF16)
        low = (value - high.astype(F32)).astype(BF16)
        span = slice(column * BLK, (column + 1) * BLK)
        rhs[slot, 0:BLK, span] = high
        rhs[slot, BLK : 2 * BLK, span] = high
        rhs[slot, 2 * BLK :, span] = low
        if column == 0:
            lhs[slot, :, 0:BLK] = high
            lhs[slot, :, BLK : 2 * BLK] = low
            lhs[slot, :, 2 * BLK :] = high

    def dot(a, b):
        return jnp.dot(a, b, preferred_element_type=F32)

    def inverses(slots):
        scale = {}
        for s in slots:
            def rows(first, count):
                return ft[s, first : first + count].astype(F32)

            mixed, turned = rows(0, 128), rows(0, 128).T
            folded = rows(512, 64)
            lines = rows(576, 16)
            square = jnp.concatenate([folded, pltpu.roll(folded, 64, 1)], axis=0)
            upright = ((row < 64) & (row <= col)) | ((row >= 64) & (col >= 64) & (row > col))
            block = {
                (0, 0): jnp.where(row <= col, mixed, turned),
                (0, 1): rows(128, 128),
                (0, 2): rows(256, 128),
                (1, 1): jnp.where(row == col, lines[0:1], jnp.where(row > col, mixed, turned)),
                (1, 2): rows(384, 128),
                (2, 2): jnp.where((row == col) & (row >= 64), lines[1:2], jnp.where(upright, square, square.T)),
            }
            for r in range(3):
                for k in range(3):
                    tile = block[r, k] if r <= k else block[k, r].T
                    acc[s, r * 128 : (r + 1) * 128, k * 128 : (k + 1) * 128] = tile
        for s in slots:
            factor = acc[s] * (1.0 / 8192.0) + DAMPING * eye
            bound = jnp.max(jnp.sum(jnp.abs(factor), axis=1, keepdims=True), axis=0, keepdims=True)
            scale[s] = 1.0 / bound
            residue = eye - factor * scale[s]
            acc[s] = eye + residue
            put(s, residue, 0)
            put(s, acc[s], 1)
        for s in slots:
            put(s, dot(lhs[s], rhs[s, :, :BLK]), 0)
        for _ in range(2):
            for s in slots:
                both = dot(lhs[s], rhs[s])
                acc[s] += both[:, BLK:]
                put(s, both[:, :BLK], 0)
                put(s, acc[s], 1)
        for s in slots:
            acc[s] += dot(lhs[s, :, : 2 * BLK], rhs[s, : 2 * BLK, BLK:])
            square = dot(lhs[s, :, :BLK], rhs[s, :BLK, :BLK]).astype(BF16)
            acc[s] += dot(square, acc[s].astype(BF16))
        return [(acc[s] * scale[s]).astype(BF16) for s in slots]

    for by in (1, 2, 3):
        send(gz.at[0:PART], ft.at[2, part(y)], h_s.at[by - 1], h_r.at[by - 1], dev(y=turn(y, by))).wait_recv()
    ginv[c] = inverses((2,))[0]
    swap = send(ginv.at[c], ginv.at[c], i_s, i_r, dev(c=other))
    swap.start()
    load_w.wait()
    for layer in (0, 1):
        for yy in range(4):
            mine = (x == x_from) & (c == layer) & (y == yy)

            @pl.when(jnp.logical_not(mine))
            def _():
                send(
                    dtot.at[0], ft.at[layer, part(yy)], e_s.at[0, 0], e_r.at[layer, yy], dev(c=other)
                ).wait_recv()
    for layer, inverse in enumerate(inverses((0, 1))):
        left[layer] = dot(inverse, wv[layer]).astype(BF16)
    swap.wait()
    for layer in (0, 1):
        out[layer] = dot(left[layer], ginv[layer]).astype(BF16)

    for copy in started:
        copy.wait_send()
    for t in range(4):
        @pl.when(z != 2 * lax.rem(x, 2) + t // 2)
        def _():
            send(cs.at[0], crec.at[0, 0], c_s.at[t], c_r.at[0, 0], dev(c=other)).wait_send()

    @pl.when(active)
    def _():
        for e in (0, 1):
            cross(e).wait_send()

    for e in (0, 1):
        for by in range(4):
            copy = send(dtot.at[0], ft.at[0, part(0)], e_s.at[e, by], e_r.at[0, 0], dev(c=other))
            if by:
                copy.wait_send()
            else:
                @pl.when((y_goal != y) | (c != e))
                def _():
                    copy.wait_send()


def shards(hidden_acts, out_grads, token_picks, weight_grads):
    dma = pltpu.SemaphoreType.DMA
    vmem = pltpu.VMEM
    return pl.pallas_call(
        kernel,
        out_shape=jax.ShapeDtypeStruct(weight_grads.shape, BF16),
        in_specs=[
            pl.BlockSpec(memory_space=pl.ANY),
            pl.BlockSpec(memory_space=pl.ANY),
            pl.BlockSpec(memory_space=vmem),
            pl.BlockSpec(memory_space=pl.ANY),
        ],
        out_specs=pl.BlockSpec(memory_space=vmem),
        scratch_shapes=[
            vmem(hidden_acts.shape, BF16), vmem(out_grads.shape, BF16), vmem(weight_grads.shape, BF16),
            vmem((POOL, BLK), BF16),
            vmem((5, ROWS, 128), BF16), vmem((5, ROWS, 128), BF16), vmem((5, ROWS, 128), F32), vmem((5, ROWS, 128), BF16),
            vmem((3, 5, PART, 128), BF16), vmem((5, PART, 128), F32), vmem((5, PART, 128), BF16),
            vmem((3, 2, PART, 128), BF16), vmem((3, SLICE, 128), BF16), vmem((2, PART, 128), BF16),
            vmem((SLICE, 128), BF16), vmem((4 * SLICE, 128), F32), vmem((4 * SLICE, 128), BF16), vmem((4 * SLICE, 128), BF16),
            vmem((3, ROWS, 128), BF16),
            vmem((3, BLK, 3 * BLK), BF16), vmem((3, 3 * BLK, 2 * BLK), BF16), vmem((3, BLK, BLK), F32),
            vmem((2, BLK, BLK), BF16), vmem((2, BLK, BLK), BF16),
            dma((11,)), dma((5,)), dma((5,)), dma((5, 3)), dma((5, 3)), dma((4,)), dma((3, 2)), dma((3,)), dma((3,)), dma((3,)), dma((3,)),
            dma((2,)), dma((2,)), dma((2, 4)), dma((2, 4)), dma((3,)), dma((3,)), dma, dma,
        ],
        compiler_params=pltpu.CompilerParams(
            collective_id=0, has_side_effects=True, vmem_limit_bytes=53 * 2**20
        ),
    )(hidden_acts, out_grads, token_picks, weight_grads)


def solution(mesh):
    placed = (P(None, "dp", "mp"), P(None, "dp", "mp"), P("dp", None), P(None, "dp", "mp"))
    return jax.shard_map(shards, mesh=mesh, in_specs=placed, out_specs=P(None, "dp", "mp"), check_vma=False)
```
